32 devices in a mesh: section: 4 (over x, core), dp: 8 (over z, y).
Axes of the slice: x: 2, y: 2, z: 4, core: 2. Of those that a mesh axis runs over, the one named last changes fastest.
Arguments:
- micro_inputs: bfloat16 [4, 512, 4096], P(None, 'dp'), may hold values from -6 to 6
- out_cotangent: bfloat16 [4, 512, 4096], P(None, 'dp'), may hold values from -0.3125 to 0.3125
- weight_a: bfloat16 [2, 4, 4096, 512], P(None, 'section'), may hold values from -0.09375 to 0.09375
- weight_b: bfloat16 [2, 4, 512, 4096], P(None, 'section'), may hold values from -0.25 to 0.25
- mask_a: int32 [2, 4, 64, 8], P(None, 'section'), may hold values from 0 to 1, as said below
- mask_b: int32 [2, 4, 8, 64], P(None, 'section'), may hold values from 0 to 1, as said below
Outputs:
- grad_a: float32 [2, 4, 4096, 512], P(None, 'section', 'dp')
- grad_b: float32 [2, 4, 512, 4096], P(None, 'section', None, 'dp')
The draws below stay inside these ranges and needn't reach their ends.
Inputs may be any that keep to these rules, and one draw needn't show every extreme that they name: Each block of a layer is kept with a probability drawn for that layer from 30 to 50 percent; mask_a and mask_b of one layer share it. `mask_b`: drawn with the same per-layer probabilities as mask_a.
All inputs are finite; a program needn't handle non-finite values.
Results may differ from the reference program's by a relative error of at most 0.033.
Values may be sent and summed in bfloat16 or wider, within the bound.
A program may use at most 192 MiB of HBM per device.

```python
import jax
import jax.numpy as jnp
from jax import lax

D = 4096
R = 512
BLK = 64
MB = 4
TOK = 64
SECTIONS = 4
TOKENS = 512
ROWS = 2048
N_DP = 8


def layer_limits(key):
    return jax.random.randint(jax.random.fold_in(key, 11), (2, SECTIONS, 1, 1), 30, 51)


def draw_mask_a(key, part):
    limits = layer_limits(key)
    picks = jax.random.randint(jax.random.fold_in(key, 21), (2, SECTIONS, D // BLK, R // BLK), 0, 100)
    return (picks < limits).astype(jnp.int32)


def draw_mask_b(key, part):
    limits = layer_limits(key)
    picks = jax.random.randint(jax.random.fold_in(key, 31), (2, SECTIONS, R // BLK, D // BLK), 0, 100)
    return (picks < limits).astype(jnp.int32)


def block_scale(key, extent, pieces, low, largest):
    level, own = 1.0, jax.random.fold_in(key, 6)
    for axis_at, shards_of in pieces:
        heights = jnp.exp(jax.random.uniform(jax.random.fold_in(own, axis_at), (shards_of,), jnp.float32, low / len(pieces), largest / len(pieces)))
        level = level * jnp.repeat(heights, extent[axis_at] // shards_of).reshape([-1 if axis == axis_at else 1 for axis in range(len(extent))])
    return level


def gaussian(rng, dims, spread, most, pieces=(), held_as=jnp.bfloat16):
    result = spread * jax.random.normal(rng, dims, jnp.float32)
    if pieces:
        result = result * block_scale(rng, dims, pieces, -0.22, 0.18)
    return jnp.clip(result, -most, most).astype(held_as)


def setup_inputs(seed: int = 0) -> dict:
    key_of = jax.random.split(jax.random.key(seed), 7)
    micro_inputs = gaussian(key_of[0], (MB, TOKENS, D), 1.0, 6.0, ((1, 8),))
    out_cotangent = gaussian(key_of[1], (MB, TOKENS, D), (ROWS ** -0.5), 0.3125, ((1, 8),))
    weight_a = gaussian(key_of[2], (2, SECTIONS, D, R), D ** -0.5, 0.09375, ((1, 4),))
    weight_b = gaussian(key_of[3], (2, SECTIONS, R, D), R ** -0.5, 0.25, ((1, 4),))
    mask_a = draw_mask_a(jax.random.fold_in(key_of[6], 71), 0)
    mask_b = draw_mask_b(jax.random.fold_in(key_of[6], 71), 0)
    return dict(micro_inputs=micro_inputs, out_cotangent=out_cotangent, weight_a=weight_a, weight_b=weight_b, mask_a=mask_a, mask_b=mask_b)


EPS = 1e-05

def expand_blocks(mask):
    return jnp.repeat(jnp.repeat(mask, BLK, axis=-2), BLK, axis=-1)

def normalize(values):
    wide = values.astype(jnp.float32)
    inverse = lax.rsqrt(lax.optimization_barrier(jnp.mean(wide * wide, axis=-1, keepdims=True)) + EPS)
    return (wide * inverse, inverse)

def forward_layer(values, eff_a, eff_b):
    scaled, inverse = normalize(values)
    preact = jnp.dot(scaled.astype(jnp.bfloat16), eff_a, preferred_element_type=jnp.float32)
    hidden = (preact * jax.nn.sigmoid(preact)).astype(jnp.bfloat16)
    mixed = values.astype(jnp.float32) + jnp.dot(hidden, eff_b, preferred_element_type=jnp.float32)
    return mixed.astype(jnp.bfloat16)

def backward_layer(values, upstream, eff_a, eff_b):
    scaled, inverse = normalize(values)
    normed = scaled.astype(jnp.bfloat16)
    preact = jnp.dot(normed, eff_a, preferred_element_type=jnp.float32)
    sigma = jax.nn.sigmoid(preact)
    hidden = (preact * sigma).astype(jnp.bfloat16)
    back_hidden = lax.dot_general(upstream, eff_b, (((1,), (1,)), ((), ())), preferred_element_type=jnp.float32)
    back_pre = (back_hidden * sigma * (1.0 + preact * (1.0 - sigma))).astype(jnp.bfloat16)
    back_norm = lax.dot_general(back_pre, eff_a, (((1,), (1,)), ((), ())), preferred_element_type=jnp.float32)
    center = lax.optimization_barrier(jnp.mean(back_norm * scaled, axis=-1, keepdims=True))
    downstream = (upstream.astype(jnp.float32) + inverse * (back_norm - scaled * center)).astype(jnp.bfloat16)
    return (downstream, normed, hidden, back_pre)

def group_sums(left, right):
    left_four = left.reshape(MB, N_DP, TOK, left.shape[-1]).astype(jnp.float32)
    right_four = right.reshape(MB, N_DP, TOK, right.shape[-1]).astype(jnp.float32)
    terms = jnp.einsum('mqtd,mqtr->qdr', left_four, right_four, precision=lax.Precision.HIGHEST)
    rounded = lax.optimization_barrier(terms.astype(jnp.bfloat16))
    return lax.optimization_barrier(jnp.sum(rounded.astype(jnp.float32), axis=0))

def reference(micro_inputs, out_cotangent, weight_a, weight_b, mask_a, mask_b):
    total_rows = MB * TOKENS
    depth = 2 * SECTIONS
    eff_a = []
    eff_b = []
    for layer_idx in range(depth):
        lap_idx = layer_idx // SECTIONS
        section_idx = layer_idx % SECTIONS
        eff_a.append(weight_a[lap_idx, section_idx] * expand_blocks(mask_a[lap_idx, section_idx]).astype(jnp.bfloat16))
        eff_b.append(weight_b[lap_idx, section_idx] * expand_blocks(mask_b[lap_idx, section_idx]).astype(jnp.bfloat16))
    values = micro_inputs.reshape(total_rows, D)
    saved = []
    for layer_idx in range(depth):
        saved.append(values)
        values = forward_layer(values, eff_a[layer_idx], eff_b[layer_idx])
    upstream = out_cotangent.reshape(total_rows, D)
    grads_a = [[None] * SECTIONS, [None] * SECTIONS]
    grads_b = [[None] * SECTIONS, [None] * SECTIONS]
    for layer_idx in range(depth - 1, -1, -1):
        lap_idx = layer_idx // SECTIONS
        section_idx = layer_idx % SECTIONS
        downstream, normed, hidden, back_pre = backward_layer(saved[layer_idx], upstream, eff_a[layer_idx], eff_b[layer_idx])
        sum_a = group_sums(normed, back_pre)
        sum_b = group_sums(upstream, hidden)
        grads_a[lap_idx][section_idx] = sum_a * expand_blocks(mask_a[lap_idx, section_idx]).astype(jnp.float32)
        grads_b[lap_idx][section_idx] = jnp.transpose(sum_b) * expand_blocks(mask_b[lap_idx, section_idx]).astype(jnp.float32)
        upstream = downstream
    grad_a = jnp.stack([jnp.stack(grads_a[0]), jnp.stack(grads_a[1])])
    grad_b = jnp.stack([jnp.stack(grads_b[0]), jnp.stack(grads_b[1])])
    return (grad_a, grad_b)
```

```python
import functools

import jax
import jax.numpy as jnp
from jax import lax
from jax.experimental import pallas as pl
from jax.experimental.pallas import tpu as pltpu
from jax.sharding import PartitionSpec as P

BLK = 64
EPS = 1e-05
CHUNKS = 4
LIMIT = 58 * 1024 * 1024
MESH = pl.DeviceIdType.MESH
NT = (((1,), (1,)), ((), ()))
F32 = jnp.float32
BF16 = jnp.bfloat16


def greet(here, sections):
    barrier = pltpu.get_barrier_semaphore()
    right = lax.rem(here + 1, sections)
    left = lax.rem(here + sections - 1, sections)
    for side in (left, right):
        pl.semaphore_signal(barrier, inc=1, device_id={"section": side}, device_id_type=MESH)
    pl.semaphore_wait(barrier, 2)
    return left, right


def mask_up(wa, lap, rows_a):
    def body(b, _):
        rows = pl.ds(pl.multiple_of(b * BLK, BLK), BLK)
        keep = rows_a[lap, pl.ds(b, 1), :].astype(BF16)
        wa[lap, rows, :] = wa[lap, rows, :] * keep
        return 0

    lax.fori_loop(0, wa.shape[1] // BLK, body, 0)


def mask_down(wb, lap, cols_b):
    def body(b, _):
        rows = pl.ds(pl.multiple_of(b * BLK, BLK), BLK)
        keep = cols_b[lap, pl.ds(b, 1), :].astype(BF16)
        wb[lap, rows, :] = wb[lap, rows, :] * keep
        return 0

    lax.fori_loop(0, wb.shape[1] // BLK, body, 0)


def chunk_copies(src, dst, sems, base):
    wide = src.shape[-1] // CHUNKS
    return [
        pltpu.make_async_copy(src.at[:, :, pl.ds(c * wide, wide)], dst.at[:, c], sems.at[base + c])
        for c in range(CHUNKS)
    ]


def forward_items(here, sections, right, wa, wb, xs, xout, ps, invs, send, recv):
    batches = xs.shape[0] // 2
    wide = xs.shape[-1]
    width = wide * CHUNKS

    def hop(i, c):
        last = here == sections - 1
        slot = jnp.minimum(i + jnp.where(last, batches, 0), 2 * batches - 1)
        return pltpu.make_async_remote_copy(
            src_ref=xout.at[i, c],
            dst_ref=xs.at[slot, c],
            send_sem=send.at[i, c],
            recv_sem=recv.at[slot, c],
            device_id={"section": right},
            device_id_type=MESH,
        )

    def landed(i, c):
        return pltpu.make_async_remote_copy(
            src_ref=xout.at[i, c],
            dst_ref=xs.at[i, c],
            send_sem=send.at[i, c],
            recv_sem=recv.at[i, c],
            device_id={"section": right},
            device_id_type=MESH,
        )

    def item(i, _):
        lap = i // batches
        from_left = (here > 0) | (lap > 0)
        go_on = (here < sections - 1) | (lap == 0)
        total = None
        square = None
        for c in range(CHUNKS):

            @pl.when(from_left)
            def _():
                landed(i, c).wait_recv()

            x = xs[i, c]
            xf = x.astype(F32)
            sq = jnp.sum(xf * xf, axis=-1, keepdims=True)
            q = jnp.dot(x, wa[lap, pl.ds(c * wide, wide), :], preferred_element_type=F32)
            total = q if total is None else total + q
            square = sq if square is None else square + sq
        inv = lax.rsqrt(square / width + EPS)
        p = total * inv
        ps[i] = p
        invs[i] = jnp.broadcast_to(inv, invs.shape[1:])

        @pl.when(go_on)
        def _():
            h = (p * jax.nn.sigmoid(p)).astype(BF16)
            for c in range(CHUNKS):
                y = jnp.dot(h, wb[lap, :, pl.ds(c * wide, wide)], preferred_element_type=F32)
                xout[i, c] = (xs[i, c].astype(F32) + y).astype(BF16)
                hop(i, c).start()

        return 0

    lax.fori_loop(0, 2 * batches, item, 0)

    def finish():
        def body(i, _):
            lap = i // batches

            @pl.when((here < sections - 1) | (lap == 0))
            def _():
                for c in range(CHUNKS):
                    hop(i, c).wait_send()

            return 0

        lax.fori_loop(0, 2 * batches, body, 0)

    return finish


def backward_items(here, sections, left, lap, base, wa, wb, xs, ps, invs, gs, gout, gpis, hs, send, recv, gnext, nsend, nrecv):
    batches = gs.shape[0]
    wide = gs.shape[-1]
    width = wide * CHUNKS

    def hop(i, c):
        return pltpu.make_async_remote_copy(
            src_ref=gout.at[i, c],
            dst_ref=gs.at[i, c],
            send_sem=send.at[i, c],
            recv_sem=recv.at[i, c],
            device_id={"section": left},
            device_id_type=MESH,
        )

    def wrap(i, c):
        return pltpu.make_async_remote_copy(
            src_ref=gout.at[i, c],
            dst_ref=gnext.at[i, c],
            send_sem=nsend.at[i, c],
            recv_sem=nrecv.at[i, c],
            device_id={"section": left},
            device_id_type=MESH,
        )

    def item(i, _):
        total = None
        for c in range(CHUNKS):

            @pl.when(here < sections - 1)
            def _():
                hop(i, c).wait_recv()

            q = lax.dot_general(
                gs[i, c], wb[lap, :, pl.ds(c * wide, wide)], NT, preferred_element_type=F32
            )
            total = q if total is None else total + q
        p = ps[base + i]
        inv = invs[base + i][:, :1]
        sg = jax.nn.sigmoid(p)
        gp = total * sg * (1.0 + p * (1.0 - sg))
        rounded = gp.astype(BF16)
        gpis[i] = gp * inv
        hs[i] = p * sg
        mean = jnp.sum(rounded.astype(F32) * p, axis=-1, keepdims=True) / width
        scale = inv * inv * mean

        def outgoing():
            for c in range(CHUNKS):
                gn = lax.dot_general(
                    rounded, wa[lap, pl.ds(c * wide, wide), :], NT, preferred_element_type=F32
                )
                out = gs[i, c].astype(F32) + inv * gn - xs[base + i, c].astype(F32) * scale
                gout[i, c] = out.astype(BF16)

                @pl.when(here > 0)
                def _():
                    hop(i, c).start()

                if gnext is not None:

                    @pl.when(here == 0)
                    def _():
                        wrap(i, c).start()

        if gnext is not None:
            outgoing()
        else:
            pl.when(here > 0)(outgoing)
        return 0

    lax.fori_loop(0, batches, item, 0)

    def finish():
        def body(i, _):
            for c in range(CHUNKS):

                @pl.when(here > 0)
                def _():
                    hop(i, c).wait_send()

                if gnext is not None:

                    @pl.when(here == 0)
                    def _():
                        wrap(i, c).wait_send()

                    @pl.when(here == sections - 1)
                    def _():
                        wrap(i, c).wait_recv()

            return 0

        lax.fori_loop(0, batches, body, 0)

    return finish


def weight_terms(base, xs, gs, gpis, hs, turned, stage, out_a, out_b, sems):
    batches = gs.shape[0]
    wide = gs.shape[-1]
    tokens = gs.shape[2]
    rows = batches * tokens
    groups, inner, span = stage.shape[1:]
    for m in range(batches):
        pass
    flat_gp = gpis[...].reshape(rows, inner)
    flat_h = hs[...].reshape(rows, inner)
    turned[0] = jnp.transpose(flat_gp).astype(BF16)
    turned[1] = jnp.transpose(flat_h).astype(BF16)
    per = wide // span
    copies = []

    def owner(c, _):
        for k in range(per):
            q = c * per + k
            cols = pl.ds(k * span, span)
            x = xs[pl.ds(base, batches), c, :, cols].reshape(rows, span)
            g = gs[:, c, :, cols].reshape(rows, span)
            stage[0, q] = jnp.dot(turned[0], x, preferred_element_type=F32).astype(BF16)
            stage[1, q] = jnp.dot(turned[1], g, preferred_element_type=F32).astype(BF16)
        return 0

    lax.fori_loop(0, CHUNKS, owner, 0)
    copies = [
        pltpu.make_async_copy(stage.at[0], out_a, sems.at[0]),
        pltpu.make_async_copy(stage.at[1], out_b, sems.at[1]),
    ]
    for copy in copies:
        copy.start()
    return copies


def first_kernel(
    sections, micro, cot, weight_a, weight_b, rows_a, cols_b,
    out_a, out_b, x_keep, p_keep, inv_keep, g_keep,
    wa, wb, xs, xout, ps, invs, gs, gout, gnext, gpis, hs, turned, stage,
    load, keep, xsend, xrecv, gsend, grecv, nsend, nrecv, out_sem,
):
    here = lax.axis_index("section")
    batches = gs.shape[0]
    loads = []
    for lap in range(2):
        loads.append(pltpu.make_async_copy(weight_a.at[lap, 0], wa.at[lap], load.at[2 * lap]))
        loads.append(pltpu.make_async_copy(weight_b.at[lap, 0], wb.at[lap], load.at[2 * lap + 1]))
    for copy in loads:
        copy.start()
    x_in = chunk_copies(micro, xs.at[pl.ds(0, batches)], load, 4)
    g_in = chunk_copies(cot, gs, load, 4 + CHUNKS)

    @pl.when(here == 0)
    def _():
        for copy in x_in:
            copy.start()

    @pl.when(here == sections - 1)
    def _():
        for copy in g_in:
            copy.start()

    left, right = greet(here, sections)
    for lap in range(2):
        loads[2 * lap].wait()
        mask_up(wa, lap, rows_a)
        loads[2 * lap + 1].wait()
        mask_down(wb, lap, cols_b)

    @pl.when(here == 0)
    def _():
        for copy in x_in:
            copy.wait()

    x_done = forward_items(here, sections, right, wa, wb, xs, xout, ps, invs, xsend, xrecv)

    @pl.when(here == sections - 1)
    def _():
        for copy in g_in:
            copy.wait()

    keeps = [
        pltpu.make_async_copy(xs.at[pl.ds(0, batches)], x_keep, keep.at[0]),
        pltpu.make_async_copy(ps.at[pl.ds(0, batches)], p_keep, keep.at[1]),
        pltpu.make_async_copy(invs.at[pl.ds(0, batches)], inv_keep, keep.at[2]),
    ]
    for copy in keeps:
        copy.start()
    g_done = backward_items(
        here, sections, left, 1, batches, wa, wb, xs, ps, invs, gs, gout, gpis, hs, gsend, grecv, gnext, nsend, nrecv
    )
    outs = weight_terms(batches, xs, gs, gpis, hs, turned, stage, out_a, out_b, out_sem)
    x_done()
    g_done()

    @pl.when(here == sections - 1)
    def _():
        copy = pltpu.make_async_copy(gnext, g_keep, keep.at[3])
        copy.start()
        copy.wait()

    for copy in keeps + outs:
        copy.wait()


def second_kernel(
    sections, x_keep, p_keep, inv_keep, g_keep, weight_a, weight_b, rows_a, cols_b,
    out_a, out_b,
    wa, wb, xs, ps, invs, gs, gout, gpis, hs, turned, stage,
    load, gsend, grecv, out_sem,
):
    here = lax.axis_index("section")
    loads = [
        pltpu.make_async_copy(weight_a.at[0, 0], wa.at[0], load.at[0]),
        pltpu.make_async_copy(weight_b.at[0, 0], wb.at[0], load.at[1]),
        pltpu.make_async_copy(x_keep, xs, load.at[2]),
        pltpu.make_async_copy(p_keep, ps, load.at[3]),
        pltpu.make_async_copy(inv_keep, invs, load.at[4]),
    ]
    for copy in loads:
        copy.start()
    g_in = pltpu.make_async_copy(g_keep, gs, load.at[5])

    @pl.when(here == sections - 1)
    def _():
        g_in.start()

    left, right = greet(here, sections)
    for copy in loads:
        copy.wait()
    mask_down(wb, 0, cols_b)
    mask_up(wa, 0, rows_a)

    @pl.when(here == sections - 1)
    def _():
        g_in.wait()

    g_done = backward_items(
        here, sections, left, 0, 0, wa, wb, xs, ps, invs, gs, gout, gpis, hs, gsend, grecv, None, None, None
    )
    outs = weight_terms(0, xs, gs, gpis, hs, turned, stage, out_a, out_b, out_sem)
    g_done()
    for copy in outs:
        copy.wait()


def expand_blocks(mask):
    return jnp.repeat(jnp.repeat(mask, BLK, axis=-2), BLK, axis=-1)


def on_device(micro_inputs, out_cotangent, weight_a, weight_b, mask_a, mask_b):
    sections = lax.axis_size("section")
    groups = lax.axis_size("dp")
    owner = lax.axis_index("dp")
    batches, tokens, width = micro_inputs.shape
    inner = weight_a.shape[3]
    span = width // groups
    wide = width // CHUNKS
    rows_a = jnp.repeat(mask_a[:, 0].astype(F32), BLK, axis=-1)
    cols_b = jnp.repeat(mask_b[:, 0].astype(F32), BLK, axis=-1)
    any_spec = pl.BlockSpec(memory_space=pl.ANY)
    vmem_spec = pl.BlockSpec(memory_space=pltpu.VMEM)
    dma = pltpu.SemaphoreType.DMA
    term = jax.ShapeDtypeStruct((groups, inner, span), BF16)
    block = (batches, CHUNKS, tokens, wide)
    flops = 2 * batches * tokens * width * inner

    def call(kernel, cid, in_specs, outs, scratch, count):
        return pl.pallas_call(
            functools.partial(kernel, sections),
            out_shape=outs,
            in_specs=in_specs,
            out_specs=tuple(any_spec for _ in outs),
            scratch_shapes=scratch,
            compiler_params=pltpu.CompilerParams(
                collective_id=cid, has_side_effects=True, vmem_limit_bytes=LIMIT
            ),
            cost_estimate=pl.CostEstimate(
                flops=count * flops, bytes_accessed=40 * 1024 * 1024, transcendentals=0
            ),
        )

    out_a1, out_b1, x0, p0, inv0, g0 = call(
        first_kernel,
        0,
        [any_spec] * 4 + [vmem_spec] * 2,
        (
            term,
            term,
            jax.ShapeDtypeStruct(block, BF16),
            jax.ShapeDtypeStruct((batches, tokens, inner), F32),
            jax.ShapeDtypeStruct((batches, tokens, 128), F32),
            jax.ShapeDtypeStruct(block, BF16),
        ),
        [
            pltpu.VMEM((2, width, inner), BF16),
            pltpu.VMEM((2, inner, width), BF16),
            pltpu.VMEM((2 * batches,) + block[1:], BF16),
            pltpu.VMEM((2 * batches,) + block[1:], BF16),
            pltpu.VMEM((2 * batches, tokens, inner), F32),
            pltpu.VMEM((2 * batches, tokens, 128), F32),
            pltpu.VMEM(block, BF16),
            pltpu.VMEM(block, BF16),
            pltpu.VMEM(block, BF16),
            pltpu.VMEM((batches, tokens, inner), F32),
            pltpu.VMEM((batches, tokens, inner), F32),
            pltpu.VMEM((2, inner, batches * tokens), BF16),
            pltpu.VMEM((2, groups, inner, span), BF16),
            dma((4 + 2 * CHUNKS,)),
            dma((4,)),
            dma((2 * batches, CHUNKS)),
            dma((2 * batches, CHUNKS)),
            dma((batches, CHUNKS)),
            dma((batches, CHUNKS)),
            dma((batches, CHUNKS)),
            dma((batches, CHUNKS)),
            dma((2,)),
        ],
        8,
    )(micro_inputs, out_cotangent, weight_a, weight_b, rows_a, cols_b)

    def settle(term_a, term_b, lap):
        sum_a = lax.psum_scatter(term_a, "dp", scatter_dimension=0, tiled=True)[0].astype(F32)
        sum_b = lax.psum_scatter(term_b, "dp", scatter_dimension=0, tiled=True)[0].astype(F32)
        held = span // BLK
        own_a = expand_blocks(lax.dynamic_slice_in_dim(mask_a[lap, 0], owner * held, held, 0))
        own_b = expand_blocks(lax.dynamic_slice_in_dim(mask_b[lap, 0], owner * held, held, 1))
        return jnp.transpose(sum_a) * own_a.astype(F32), sum_b * own_b.astype(F32)

    later_one = settle(out_a1, out_b1, 1)
    out_a0, out_b0 = call(
        second_kernel,
        1,
        [any_spec] * 6 + [vmem_spec] * 2,
        (term, term),
        [
            pltpu.VMEM((1, width, inner), BF16),
            pltpu.VMEM((1, inner, width), BF16),
            pltpu.VMEM(block, BF16),
            pltpu.VMEM((batches, tokens, inner), F32),
            pltpu.VMEM((batches, tokens, 128), F32),
            pltpu.VMEM(block, BF16),
            pltpu.VMEM(block, BF16),
            pltpu.VMEM((batches, tokens, inner), F32),
            pltpu.VMEM((batches, tokens, inner), F32),
            pltpu.VMEM((2, inner, batches * tokens), BF16),
            pltpu.VMEM((2, groups, inner, span), BF16),
            dma((6,)),
            dma((batches, CHUNKS)),
            dma((batches, CHUNKS)),
            dma((2,)),
        ],
        4,
    )(x0, p0, inv0, g0, weight_a, weight_b, rows_a, cols_b)
    later_zero = settle(out_a0, out_b0, 0)
    grad_a = jnp.stack([later_zero[0], later_one[0]])[:, None]
    grad_b = jnp.stack([later_zero[1], later_one[1]])[:, None]
    return (grad_a, grad_b)


def solution(mesh):
    placed = (
        P(None, "dp", None),
        P(None, "dp", None),
        P(None, "section", None, None),
        P(None, "section", None, None),
        P(None, "section", None, None),
        P(None, "section", None, None),
    )
    return jax.shard_map(
        on_device,
        mesh=mesh,
        in_specs=placed,
        out_specs=(P(None, "section", "dp", None), P(None, "section", None, "dp")),
        check_vma=False,
    )
```

```python
import functools

import jax
import jax.numpy as jnp
from jax import lax
from jax.experimental import pallas as pl
from jax.experimental.pallas import tpu as pltpu
from jax.sharding import PartitionSpec as P

BLK = 64
EPS = 1e-05
CHUNKS = 4
LIMIT = 58 * 1024 * 1024
MESH = pl.DeviceIdType.MESH
NT = (((1,), (1,)), ((), ()))
F32 = jnp.float32
BF16 = jnp.bfloat16


def greet(here, sections):
    barrier = pltpu.get_barrier_semaphore()
    right = lax.rem(here + 1, sections)
    left = lax.rem(here + sections - 1, sections)
    for side in (left, right):
        pl.semaphore_signal(barrier, inc=1, device_id={"section": side}, device_id_type=MESH)
    pl.semaphore_wait(barrier, 2)
    return left, right


def mask_up(wa, lap, rows_a):
    def body(b, _):
        rows = pl.ds(pl.multiple_of(b * BLK, BLK), BLK)
        keep = rows_a[lap, pl.ds(b, 1), :].astype(BF16)
        wa[lap, rows, :] = wa[lap, rows, :] * keep
        return 0

    lax.fori_loop(0, wa.shape[1] // BLK, body, 0)


def mask_down(wb, lap, cols_b):
    def body(b, _):
        rows = pl.ds(pl.multiple_of(b * BLK, BLK), BLK)
        keep = cols_b[lap, pl.ds(b, 1), :].astype(BF16)
        wb[lap, rows, :] = wb[lap, rows, :] * keep
        return 0

    lax.fori_loop(0, wb.shape[1] // BLK, body, 0)


def chunk_copies(src, dst, sems, base):
    wide = src.shape[-1] // CHUNKS
    return [
        pltpu.make_async_copy(src.at[:, :, pl.ds(c * wide, wide)], dst.at[:, c], sems.at[base + c])
        for c in range(CHUNKS)
    ]


def forward_items(here, sections, right, wa, wb, xs, xout, ps, invs, send, recv):
    batches = xs.shape[0] // 2
    wide = xs.shape[-1]
    width = wide * CHUNKS

    def hop(i, c):
        last = here == sections - 1
        slot = jnp.minimum(i + jnp.where(last, batches, 0), 2 * batches - 1)
        return pltpu.make_async_remote_copy(
            src_ref=xout.at[i, c],
            dst_ref=xs.at[slot, c],
            send_sem=send.at[i, c],
            recv_sem=recv.at[slot, c],
            device_id={"section": right},
            device_id_type=MESH,
        )

    def landed(i, c):
        return pltpu.make_async_remote_copy(
            src_ref=xout.at[i, c],
            dst_ref=xs.at[i, c],
            send_sem=send.at[i, c],
            recv_sem=recv.at[i, c],
            device_id={"section": right},
            device_id_type=MESH,
        )

    def item(i, _):
        lap = i // batches
        from_left = (here > 0) | (lap > 0)
        go_on = (here < sections - 1) | (lap == 0)
        total = None
        square = None
        for c in range(CHUNKS):

            @pl.when(from_left)
            def _():
                landed(i, c).wait_recv()

            x = xs[i, c]
            xf = x.astype(F32)
            sq = jnp.sum(xf * xf, axis=-1, keepdims=True)
            q = jnp.dot(x, wa[lap, pl.ds(c * wide, wide), :], preferred_element_type=F32)
            total = q if total is None else total + q
            square = sq if square is None else square + sq
        inv = lax.rsqrt(square / width + EPS)
        p = total * inv
        ps[i] = p
        invs[i] = jnp.broadcast_to(inv, invs.shape[1:])

        @pl.when(go_on)
        def _():
            h = (p * jax.nn.sigmoid(p)).astype(BF16)
            for c in range(CHUNKS):
                y = jnp.dot(h, wb[lap, :, pl.ds(c * wide, wide)], preferred_element_type=F32)
                xout[i, c] = (xs[i, c].astype(F32) + y).astype(BF16)
                hop(i, c).start()

        return 0

    lax.fori_loop(0, 2 * batches, item, 0)

    def finish():
        def body(i, _):
            lap = i // batches

            @pl.when((here < sections - 1) | (lap == 0))
            def _():
                for c in range(CHUNKS):
                    hop(i, c).wait_send()

            return 0

        lax.fori_loop(0, 2 * batches, body, 0)

    return finish


def backward_items(here, sections, left, lap, base, wa, wb, xs, ps, invs, gs, gout, gpis, hs, send, recv, gnext, nsend, nrecv):
    batches = gs.shape[0]
    wide = gs.shape[-1]
    width = wide * CHUNKS

    def hop(i, c):
        return pltpu.make_async_remote_copy(
            src_ref=gout.at[i, c],
            dst_ref=gs.at[i, c],
            send_sem=send.at[i, c],
            recv_sem=recv.at[i, c],
            device_id={"section": left},
            device_id_type=MESH,
        )

    def wrap(i, c):
        return pltpu.make_async_remote_copy(
            src_ref=gout.at[i, c],
            dst_ref=gnext.at[i, c],
            send_sem=nsend.at[i, c],
            recv_sem=nrecv.at[i, c],
            device_id={"section": left},
            device_id_type=MESH,
        )

    def item(i, _):
        total = None
        for c in range(CHUNKS):

            @pl.when(here < sections - 1)
            def _():
                hop(i, c).wait_recv()

            q = lax.dot_general(
                gs[i, c], wb[lap, :, pl.ds(c * wide, wide)], NT, preferred_element_type=F32
            )
            total = q if total is None else total + q
        p = ps[base + i]
        inv = invs[base + i][:, :1]
        sg = jax.nn.sigmoid(p)
        gp = total * sg * (1.0 + p * (1.0 - sg))
        rounded = gp.astype(BF16)
        gpis[i] = gp * inv
        hs[i] = p * sg
        mean = jnp.sum(rounded.astype(F32) * p, axis=-1, keepdims=True) / width
        scale = inv * inv * mean

        def outgoing():
            for c in range(CHUNKS):
                gn = lax.dot_general(
                    rounded, wa[lap, pl.ds(c * wide, wide), :], NT, preferred_element_type=F32
                )
                out = gs[i, c].astype(F32) + inv * gn - xs[base + i, c].astype(F32) * scale
                gout[i, c] = out.astype(BF16)

                @pl.when(here > 0)
                def _():
                    hop(i, c).start()

                if gnext is not None:

                    @pl.when(here == 0)
                    def _():
                        wrap(i, c).start()

        if gnext is not None:
            outgoing()
        else:
            pl.when(here > 0)(outgoing)
        return 0

    def finish():
        def body(i, _):
            for c in range(CHUNKS):

                @pl.when(here > 0)
                def _():
                    hop(i, c).wait_send()

                if gnext is not None:

                    @pl.when(here == 0)
                    def _():
                        wrap(i, c).wait_send()

                    @pl.when(here == sections - 1)
                    def _():
                        wrap(i, c).wait_recv()

            return 0

        lax.fori_loop(0, batches, body, 0)

    return item, finish


def weight_terms(base, xs, gs, gpis, hs, turned, stage):
    batches = gs.shape[0]
    wide = gs.shape[-1]
    tokens = gs.shape[2]
    rows = batches * tokens
    groups, inner, span = stage.shape[1:]
    flat_gp = gpis[...].reshape(rows, inner)
    flat_h = hs[...].reshape(rows, inner)
    turned[0] = jnp.transpose(flat_gp).astype(BF16)
    turned[1] = jnp.transpose(flat_h).astype(BF16)
    per = wide // span

    def owner(c, _):
        for k in range(per):
            q = c * per + k
            cols = pl.ds(k * span, span)
            x = xs[pl.ds(base, batches), c, :, cols].reshape(rows, span)
            g = gs[:, c, :, cols].reshape(rows, span)
            stage[0, q] = jnp.dot(turned[0], x, preferred_element_type=F32).astype(BF16)
            stage[1, q] = jnp.dot(turned[1], g, preferred_element_type=F32).astype(BF16)
        return 0

    lax.fori_loop(0, CHUNKS, owner, 0)


def ring(me, groups, stage, slots, sends, recvs):
    half = stage.shape[2] // 2
    place = jnp.where(me % 2 == 0, me // 2, groups - 1 - me // 2)

    def device_at(spot):
        return jnp.where(spot < groups // 2, 2 * spot, 2 * (groups - 1 - spot) + 1)

    def peer(way):
        return device_at(lax.rem(place + (1 if way == 0 else groups - 1), groups))

    def own(way, part, k):
        spot = place + 2 * groups - 1 - k if way == 0 else place + 1 + k
        return stage.at[part, device_at(lax.rem(spot, groups)), pl.ds(way * half, half)]

    def hop(way, part, k):
        return pltpu.make_async_remote_copy(
            src_ref=slots.at[way, jnp.maximum(k - 1, 0), part],
            dst_ref=slots.at[way, k, part],
            send_sem=sends.at[way, k, part],
            recv_sem=recvs.at[way, k, part],
            device_id={"dp": peer(way)},
            device_id_type=MESH,
        )

    def first(way, part):
        return pltpu.make_async_remote_copy(
            src_ref=own(way, part, 0),
            dst_ref=slots.at[way, 0, part],
            send_sem=sends.at[way, 0, part],
            recv_sem=recvs.at[way, 0, part],
            device_id={"dp": peer(way)},
            device_id_type=MESH,
        )

    pairs = [(way, part) for part in range(2) for way in range(2)]

    def begin():
        for way, part in pairs:
            first(way, part).start()

    def step(k):
        for way, part in pairs:
            hop(way, part, k - 1).wait_recv()
            term = own(way, part, k)[...].astype(F32)
            slot = slots.at[way, k - 1, part]
            slot[...] = (slot[...].astype(F32) + term).astype(BF16)
            hop(way, part, k).start()

    def end(total):
        for way, part in pairs:
            hop(way, part, groups - 2).wait_recv()
            term = own(way, part, groups - 1)[...].astype(F32)
            total[part, pl.ds(way * half, half)] = (
                slots[way, groups - 2, part].astype(F32) + term
            )

    def drain():
        for way, part in pairs:
            first(way, part).wait_send()

        def body(k, _):
            for way, part in pairs:
                hop(way, part, k).wait_send()
            return 0

        lax.fori_loop(1, groups - 1, body, 0)

    return begin, step, end, drain


def first_kernel(
    sections, micro, cot, weight_a, weight_b, rows_a, cols_b,
    out, x_keep, p_keep, inv_keep, g_keep,
    wa, wb, xs, xout, ps, invs, gs, gout, gnext, gpis, hs, turned, stage,
    load, keep, xsend, xrecv, gsend, grecv, nsend, nrecv, out_sem,
):
    here = lax.axis_index("section")
    batches = gs.shape[0]
    loads = []
    for lap in range(2):
        loads.append(pltpu.make_async_copy(weight_a.at[lap, 0], wa.at[lap], load.at[2 * lap]))
        loads.append(pltpu.make_async_copy(weight_b.at[lap, 0], wb.at[lap], load.at[2 * lap + 1]))
    for copy in loads:
        copy.start()
    x_in = chunk_copies(micro, xs.at[pl.ds(0, batches)], load, 4)
    g_in = chunk_copies(cot, gs, load, 4 + CHUNKS)

    @pl.when(here == 0)
    def _():
        for copy in x_in:
            copy.start()

    @pl.when(here == sections - 1)
    def _():
        for copy in g_in:
            copy.start()

    left, right = greet(here, sections)
    for lap in range(2):
        loads[2 * lap].wait()
        mask_up(wa, lap, rows_a)
        loads[2 * lap + 1].wait()
        mask_down(wb, lap, cols_b)

    @pl.when(here == 0)
    def _():
        for copy in x_in:
            copy.wait()

    x_done = forward_items(here, sections, right, wa, wb, xs, xout, ps, invs, xsend, xrecv)

    @pl.when(here == sections - 1)
    def _():
        for copy in g_in:
            copy.wait()

    keeps = [
        pltpu.make_async_copy(xs.at[pl.ds(0, batches)], x_keep, keep.at[0]),
        pltpu.make_async_copy(ps.at[pl.ds(0, batches)], p_keep, keep.at[1]),
        pltpu.make_async_copy(invs.at[pl.ds(0, batches)], inv_keep, keep.at[2]),
    ]
    for copy in keeps:
        copy.start()
    item, g_done = backward_items(
        here, sections, left, 1, batches, wa, wb, xs, ps, invs, gs, gout, gpis, hs, gsend, grecv, gnext, nsend, nrecv
    )
    lax.fori_loop(0, batches, item, 0)
    weight_terms(batches, xs, gs, gpis, hs, turned, stage)
    outs = [pltpu.make_async_copy(stage, out, out_sem.at[0])]
    outs[0].start()
    x_done()
    g_done()

    @pl.when(here == sections - 1)
    def _():
        copy = pltpu.make_async_copy(gnext, g_keep, keep.at[3])
        copy.start()
        copy.wait()

    for copy in keeps + outs:
        copy.wait()


def second_kernel(
    sections, groups, term_one, x_keep, p_keep, inv_keep, g_keep, weight_a, weight_b, rows_a, cols_b,
    out,
    wa, wb, xs, ps, invs, gs, gout, gpis, hs, turned, stage, later, slots, late_slots, totals,
    load, gsend, grecv, rsend, rrecv, late_send, late_recv, out_sem,
):
    here = lax.axis_index("section")
    me = lax.axis_index("dp")
    batches = gs.shape[0]
    term_in = pltpu.make_async_copy(term_one, later, load.at[6])
    term_in.start()
    loads = [
        pltpu.make_async_copy(weight_b.at[0, 0], wb.at[0], load.at[1]),
        pltpu.make_async_copy(weight_a.at[0, 0], wa.at[0], load.at[0]),
        pltpu.make_async_copy(x_keep, xs, load.at[2]),
        pltpu.make_async_copy(p_keep, ps, load.at[3]),
        pltpu.make_async_copy(inv_keep, invs, load.at[4]),
    ]
    for copy in loads:
        copy.start()
    g_in = pltpu.make_async_copy(g_keep, gs, load.at[5])

    @pl.when(here == sections - 1)
    def _():
        g_in.start()

    barrier = pltpu.get_barrier_semaphore()
    place = jnp.where(me % 2 == 0, me // 2, groups - 1 - me // 2)
    left = lax.rem(here + sections - 1, sections)
    for away in (1, groups - 1):
        spot = lax.rem(place + away, groups)
        other = jnp.where(spot < groups // 2, 2 * spot, 2 * (groups - 1 - spot) + 1)
        pl.semaphore_signal(barrier, inc=1, device_id={"dp": other}, device_id_type=MESH)
    for away in (1, sections - 1):
        other = lax.rem(here + away, sections)
        pl.semaphore_signal(barrier, inc=1, device_id={"section": other}, device_id_type=MESH)
    pl.semaphore_wait(barrier, 4)
    late_begin, late_step, late_end, late_drain = ring(
        me, groups, later, late_slots, late_send, late_recv
    )
    begin, step, end, drain = ring(me, groups, stage, slots, rsend, rrecv)
    term_in.wait()
    late_begin()
    for copy in loads:
        copy.wait()
    mask_down(wb, 0, cols_b)
    mask_up(wa, 0, rows_a)

    @pl.when(here == sections - 1)
    def _():
        g_in.wait()

    item, g_done = backward_items(
        here, sections, left, 0, 0, wa, wb, xs, ps, invs, gs, gout, gpis, hs, gsend, grecv, None, None, None
    )
    turns = batches + sections - 1

    def turn(t, _):
        i = t - (sections - 1 - here)

        @pl.when((i >= 0) & (i < batches))
        def _():
            item(jnp.clip(i, 0, batches - 1), 0)

        @pl.when(t + 1 <= groups - 2)
        def _():
            late_step(jnp.minimum(t + 1, groups - 2))

        return 0

    lax.fori_loop(0, turns, turn, 0)
    for k in range(turns + 1, groups - 1):
        late_step(jnp.int32(k))
    weight_terms(0, xs, gs, gpis, hs, turned, stage)
    begin()
    late_end(totals.at[1])

    def walk(k, _):
        step(k)
        return 0

    lax.fori_loop(1, groups - 1, walk, 0)
    end(totals.at[0])
    copy = pltpu.make_async_copy(totals, out, out_sem.at[0])
    copy.start()
    g_done()
    late_drain()
    drain()
    copy.wait()


def expand_blocks(mask):
    return jnp.repeat(jnp.repeat(mask, BLK, axis=-2), BLK, axis=-1)


def on_device(micro_inputs, out_cotangent, weight_a, weight_b, mask_a, mask_b):
    sections = lax.axis_size("section")
    groups = lax.axis_size("dp")
    owner = lax.axis_index("dp")
    batches, tokens, width = micro_inputs.shape
    inner = weight_a.shape[3]
    span = width // groups
    wide = width // CHUNKS
    rows_a = jnp.repeat(mask_a[:, 0].astype(F32), BLK, axis=-1)
    cols_b = jnp.repeat(mask_b[:, 0].astype(F32), BLK, axis=-1)
    any_spec = pl.BlockSpec(memory_space=pl.ANY)
    vmem_spec = pl.BlockSpec(memory_space=pltpu.VMEM)
    dma = pltpu.SemaphoreType.DMA
    term = jax.ShapeDtypeStruct((2, groups, inner, span), BF16)
    block = (batches, CHUNKS, tokens, wide)
    flops = 2 * batches * tokens * width * inner

    def call(kernel, cid, in_specs, outs, scratch, count):
        return pl.pallas_call(
            kernel,
            out_shape=outs,
            in_specs=in_specs,
            out_specs=tuple(any_spec for _ in outs),
            scratch_shapes=scratch,
            compiler_params=pltpu.CompilerParams(
                collective_id=cid, has_side_effects=True, vmem_limit_bytes=LIMIT
            ),
            cost_estimate=pl.CostEstimate(
                flops=count * flops, bytes_accessed=40 * 1024 * 1024, transcendentals=0
            ),
        )

    term_one, x0, p0, inv0, g0 = call(
        functools.partial(first_kernel, sections),
        0,
        [any_spec] * 4 + [vmem_spec] * 2,
        (
            term,
            jax.ShapeDtypeStruct(block, BF16),
            jax.ShapeDtypeStruct((batches, tokens, inner), F32),
            jax.ShapeDtypeStruct((batches, tokens, 128), F32),
            jax.ShapeDtypeStruct(block, BF16),
        ),
        [
            pltpu.VMEM((2, width, inner), BF16),
            pltpu.VMEM((2, inner, width), BF16),
            pltpu.VMEM((2 * batches,) + block[1:], BF16),
            pltpu.VMEM((2 * batches,) + block[1:], BF16),
            pltpu.VMEM((2 * batches, tokens, inner), F32),
            pltpu.VMEM((2 * batches, tokens, 128), F32),
            pltpu.VMEM(block, BF16),
            pltpu.VMEM(block, BF16),
            pltpu.VMEM(block, BF16),
            pltpu.VMEM((batches, tokens, inner), F32),
            pltpu.VMEM((batches, tokens, inner), F32),
            pltpu.VMEM((2, inner, batches * tokens), BF16),
            pltpu.VMEM((2, groups, inner, span), BF16),
            dma((4 + 2 * CHUNKS,)),
            dma((4,)),
            dma((2 * batches, CHUNKS)),
            dma((2 * batches, CHUNKS)),
            dma((batches, CHUNKS)),
            dma((batches, CHUNKS)),
            dma((batches, CHUNKS)),
            dma((batches, CHUNKS)),
            dma((2,)),
        ],
        8,
    )(micro_inputs, out_cotangent, weight_a, weight_b, rows_a, cols_b)

    ring_slots = (2, groups - 1, 2, inner // 2, span)
    (totals,) = call(
        functools.partial(second_kernel, sections, groups),
        1,
        [any_spec] * 7 + [vmem_spec] * 2,
        (jax.ShapeDtypeStruct((2, 2, inner, span), F32),),
        [
            pltpu.VMEM((1, width, inner), BF16),
            pltpu.VMEM((1, inner, width), BF16),
            pltpu.VMEM(block, BF16),
            pltpu.VMEM((batches, tokens, inner), F32),
            pltpu.VMEM((batches, tokens, 128), F32),
            pltpu.VMEM(block, BF16),
            pltpu.VMEM(block, BF16),
            pltpu.VMEM((batches, tokens, inner), F32),
            pltpu.VMEM((batches, tokens, inner), F32),
            pltpu.VMEM((2, inner, batches * tokens), BF16),
            pltpu.VMEM((2, groups, inner, span), BF16),
            pltpu.VMEM((2, groups, inner, span), BF16),
            pltpu.VMEM(ring_slots, BF16),
            pltpu.VMEM(ring_slots, BF16),
            pltpu.VMEM((2, 2, inner, span), F32),
            dma((7,)),
            dma((batches, CHUNKS)),
            dma((batches, CHUNKS)),
            dma(ring_slots[:3]),
            dma(ring_slots[:3]),
            dma(ring_slots[:3]),
            dma(ring_slots[:3]),
            dma((1,)),
        ],
        4,
    )(term_one, x0, p0, inv0, g0, weight_a, weight_b, rows_a, cols_b)

    def settle(lap):
        held = span // BLK
        own_a = expand_blocks(lax.dynamic_slice_in_dim(mask_a[lap, 0], owner * held, held, 0))
        own_b = expand_blocks(lax.dynamic_slice_in_dim(mask_b[lap, 0], owner * held, held, 1))
        return jnp.transpose(totals[lap, 0]) * own_a.astype(F32), totals[lap, 1] * own_b.astype(F32)

    later_zero = settle(0)
    later_one = settle(1)
    grad_a = jnp.stack([later_zero[0], later_one[0]])[:, None]
    grad_b = jnp.stack([later_zero[1], later_one[1]])[:, None]
    return (grad_a, grad_b)


def solution(mesh):
    placed = (
        P(None, "dp", None),
        P(None, "dp", None),
        P(None, "section", None, None),
        P(None, "section", None, None),
        P(None, "section", None, None),
        P(None, "section", None, None),
    )
    return jax.shard_map(
        on_device,
        mesh=mesh,
        in_specs=placed,
        out_specs=(P(None, "section", "dp", None), P(None, "section", None, "dp")),
        check_vma=False,
    )
```

```python
import functools

import jax
import jax.numpy as jnp
from jax import lax
from jax.experimental import pallas as pl
from jax.experimental.pallas import tpu as pltpu
from jax.sharding import PartitionSpec as P

BLK = 64
EPS = 1e-05
CHUNKS = 4
LIMIT = 64 * 1024 * 1024 - 64 * 1024
MESH = pl.DeviceIdType.MESH
NT = (((1,), (1,)), ((), ()))
F32 = jnp.float32
BF16 = jnp.bfloat16


def mask_up(wa, lap, rows_a):
    def body(b, _):
        rows = pl.ds(pl.multiple_of(b * BLK, BLK), BLK)
        keep = rows_a[lap, pl.ds(b, 1), :].astype(BF16)
        wa[lap, rows, :] = wa[lap, rows, :] * keep
        return 0

    lax.fori_loop(0, wa.shape[1] // BLK, body, 0)


def mask_down(wb, lap, cols_b):
    def body(b, _):
        rows = pl.ds(pl.multiple_of(b * BLK, BLK), BLK)
        keep = cols_b[lap, pl.ds(b, 1), :].astype(BF16)
        wb[lap, rows, :] = wb[lap, rows, :] * keep
        return 0

    lax.fori_loop(0, wb.shape[1] // BLK, body, 0)


def chunk_copies(src, dst, sems, base):
    wide = src.shape[-1] // CHUNKS
    return [
        pltpu.make_async_copy(src.at[:, :, pl.ds(c * wide, wide)], dst.at[:, c], sems.at[base + c])
        for c in range(CHUNKS)
    ]


def forward_items(here, sections, right, prepare, wa, wb, xs, xout, ps, invs, send, recv):
    batches = xs.shape[0] // 2
    wide = xs.shape[-1]
    width = wide * CHUNKS

    def hop(i, c):
        last = here == sections - 1
        slot = jnp.minimum(i + jnp.where(last, batches, 0), 2 * batches - 1)
        return pltpu.make_async_remote_copy(
            src_ref=xout.at[i, c],
            dst_ref=xs.at[slot, c],
            send_sem=send.at[i, c],
            recv_sem=recv.at[slot, c],
            device_id={"section": right},
            device_id_type=MESH,
        )

    def landed(i, c):
        return pltpu.make_async_remote_copy(
            src_ref=xout.at[i, c],
            dst_ref=xs.at[i, c],
            send_sem=send.at[i, c],
            recv_sem=recv.at[i, c],
            device_id={"section": right},
            device_id_type=MESH,
        )

    def item(i, _):
        lap = i // batches
        from_left = (here > 0) | (lap > 0)
        go_on = (here < sections - 1) | (lap == 0)

        @pl.when((here == 0) & (i == batches))
        def _():
            prepare()

        total = None
        square = None
        for c in range(CHUNKS):

            @pl.when(from_left)
            def _():
                landed(i, c).wait_recv()

            x = xs[i, c]
            xf = x.astype(F32)
            sq = jnp.sum(xf * xf, axis=-1, keepdims=True)
            q = jnp.dot(x, wa[lap, pl.ds(c * wide, wide), :], preferred_element_type=F32)
            total = q if total is None else total + q
            square = sq if square is None else square + sq
        inv = lax.rsqrt(square / width + EPS)
        p = total * inv
        ps[i] = p
        invs[i] = jnp.broadcast_to(inv, invs.shape[1:])

        @pl.when(go_on)
        def _():
            h = (p * jax.nn.sigmoid(p)).astype(BF16)
            for c in range(CHUNKS):
                y = jnp.dot(h, wb[lap, :, pl.ds(c * wide, wide)], preferred_element_type=F32)
                xout[i, c] = (xs[i, c].astype(F32) + y).astype(BF16)
                hop(i, c).start()

        return 0

    lax.fori_loop(0, 2 * batches, item, 0)

    def finish():
        def body(i, _):
            lap = i // batches

            @pl.when((here < sections - 1) | (lap == 0))
            def _():
                for c in range(CHUNKS):
                    hop(i, c).wait_send()

            return 0

        lax.fori_loop(0, 2 * batches, body, 0)

    return finish


def backward_items(here, sections, left, lap, wa, wb, xs, ps, invs, gs, gout, gpis, hs, send, recv):
    batches = gpis.shape[0]
    wide = gs.shape[-1]
    width = wide * CHUNKS
    base = lap * batches

    def hop(i, c):
        slot = base + i
        if lap:
            slot = slot - jnp.where(here == 0, batches, 0)
        return pltpu.make_async_remote_copy(
            src_ref=gout.at[base + i, c],
            dst_ref=gs.at[slot, c],
            send_sem=send.at[base + i, c],
            recv_sem=recv.at[slot, c],
            device_id={"section": left},
            device_id_type=MESH,
        )

    def landed(i, c):
        return pltpu.make_async_remote_copy(
            src_ref=gout.at[base + i, c],
            dst_ref=gs.at[base + i, c],
            send_sem=send.at[base + i, c],
            recv_sem=recv.at[base + i, c],
            device_id={"section": left},
            device_id_type=MESH,
        )

    def item(i, _):
        total = None
        for c in range(CHUNKS):
            if lap:

                @pl.when(here < sections - 1)
                def _():
                    landed(i, c).wait_recv()

            else:
                landed(i, c).wait_recv()
            q = lax.dot_general(
                gs[base + i, c], wb[lap, :, pl.ds(c * wide, wide)], NT, preferred_element_type=F32
            )
            total = q if total is None else total + q
        p = ps[base + i]
        inv = invs[base + i][:, :1]
        sg = jax.nn.sigmoid(p)
        gp = total * sg * (1.0 + p * (1.0 - sg))
        rounded = gp.astype(BF16)
        gpis[i] = (gp * inv).astype(BF16)
        hs[i] = (p * sg).astype(BF16)
        mean = jnp.sum(rounded.astype(F32) * p, axis=-1, keepdims=True) / width
        scale = inv * inv * mean

        def outgoing():
            for c in range(CHUNKS):
                gn = lax.dot_general(
                    rounded, wa[lap, pl.ds(c * wide, wide), :], NT, preferred_element_type=F32
                )
                out = gs[base + i, c].astype(F32) + inv * gn - xs[base + i, c].astype(F32) * scale
                gout[base + i, c] = out.astype(BF16)
                hop(i, c).start()

        if lap:
            outgoing()
        else:
            pl.when(here > 0)(outgoing)
        return 0

    def finish():
        def body(i, _):
            for c in range(CHUNKS):
                if lap:
                    hop(i, c).wait_send()
                else:

                    @pl.when(here > 0)
                    def _():
                        hop(i, c).wait_send()

            return 0

        lax.fori_loop(0, batches, body, 0)

    return item, finish


def weight_terms(base, xs, gs, gpis, hs, turned, stage):
    batches = gpis.shape[0]
    wide = gs.shape[-1]
    tokens = gs.shape[2]
    rows = batches * tokens
    groups, inner, span = stage.shape[1:]
    per = wide // span
    for part, (left, right) in enumerate(((gpis, xs), (hs, gs))):
        turned[...] = jnp.transpose(left[...].astype(F32).reshape(rows, inner)).astype(BF16)

        def owner(c, _):
            for k in range(per):
                block = right[pl.ds(base, batches), c, :, pl.ds(k * span, span)].reshape(rows, span)
                stage[part, c * per + k] = jnp.dot(
                    turned[...], block, preferred_element_type=F32
                ).astype(BF16)
            return 0

        lax.fori_loop(0, CHUNKS, owner, 0)


def ring(me, groups, stage, slots, sends, recvs):
    half = stage.shape[2] // 2
    place = jnp.where(me % 2 == 0, me // 2, groups - 1 - me // 2)

    def device_at(spot):
        return jnp.where(spot < groups // 2, 2 * spot, 2 * (groups - 1 - spot) + 1)

    def peer(way):
        return device_at(lax.rem(place + (1 if way == 0 else groups - 1), groups))

    def own(way, part, k):
        spot = place + 2 * groups - 1 - k if way == 0 else place + 1 + k
        return stage.at[part, device_at(lax.rem(spot, groups)), pl.ds(way * half, half)]

    def hop(way, part, k):
        return pltpu.make_async_remote_copy(
            src_ref=slots.at[way, jnp.maximum(k - 1, 0), part],
            dst_ref=slots.at[way, k, part],
            send_sem=sends.at[way, k, part],
            recv_sem=recvs.at[way, k, part],
            device_id={"dp": peer(way)},
            device_id_type=MESH,
        )

    def first(way, part):
        return pltpu.make_async_remote_copy(
            src_ref=own(way, part, 0),
            dst_ref=slots.at[way, 0, part],
            send_sem=sends.at[way, 0, part],
            recv_sem=recvs.at[way, 0, part],
            device_id={"dp": peer(way)},
            device_id_type=MESH,
        )

    pairs = [(way, part) for part in range(2) for way in range(2)]

    def begin():
        for way, part in pairs:
            first(way, part).start()

    def step(k):
        for way, part in pairs:
            hop(way, part, k - 1).wait_recv()
            term = own(way, part, k)[...].astype(F32)
            slot = slots.at[way, k - 1, part]
            slot[...] = (slot[...].astype(F32) + term).astype(BF16)
            hop(way, part, k).start()

    def end(total):
        for way, part in pairs:
            hop(way, part, groups - 2).wait_recv()
            term = own(way, part, groups - 1)[...].astype(F32)
            total[part, pl.ds(way * half, half)] = (
                slots[way, groups - 2, part].astype(F32) + term
            )

    def drain():
        for way, part in pairs:
            first(way, part).wait_send()

        def body(k, _):
            for way, part in pairs:
                hop(way, part, k).wait_send()
            return 0

        lax.fori_loop(1, groups - 1, body, 0)

    return begin, step, end, drain


def whole_kernel(
    sections, groups, micro, cot, weight_a, weight_b, rows_a, cols_b,
    out,
    wa, wb, xs, xout, ps, invs, gs, gpis, hs, turned, stage, later, slots, late_slots, totals,
    load, xsend, xrecv, gsend, grecv, rsend, rrecv, late_send, late_recv, out_sem,
):
    here = lax.axis_index("section")
    me = lax.axis_index("dp")
    batches = gpis.shape[0]
    loads = []
    for lap in range(2):
        loads.append(pltpu.make_async_copy(weight_a.at[lap, 0], wa.at[lap], load.at[2 * lap]))
        loads.append(pltpu.make_async_copy(weight_b.at[lap, 0], wb.at[lap], load.at[2 * lap + 1]))
    x_in = chunk_copies(micro, xs.at[pl.ds(0, batches)], load, 4)
    g_in = chunk_copies(cot, gs.at[pl.ds(batches, batches)], load, 4 + CHUNKS)
    loads[0].start()

    @pl.when(here == 0)
    def _():
        for copy in x_in:
            copy.start()

    for copy in loads[1:]:
        copy.start()

    @pl.when(here == sections - 1)
    def _():
        for copy in g_in:
            copy.start()

    barrier = pltpu.get_barrier_semaphore()
    place = jnp.where(me % 2 == 0, me // 2, groups - 1 - me // 2)
    right = lax.rem(here + 1, sections)
    left = lax.rem(here + sections - 1, sections)
    for away in (1, groups - 1):
        spot = lax.rem(place + away, groups)
        other = jnp.where(spot < groups // 2, 2 * spot, 2 * (groups - 1 - spot) + 1)
        pl.semaphore_signal(barrier, inc=1, device_id={"dp": other}, device_id_type=MESH)
    for other in (left, right):
        pl.semaphore_signal(barrier, inc=1, device_id={"section": other}, device_id_type=MESH)
    pl.semaphore_wait(barrier, 4)

    def prepare(lap):
        loads[2 * lap].wait()
        mask_up(wa, lap, rows_a)
        loads[2 * lap + 1].wait()
        mask_down(wb, lap, cols_b)

    prepare(0)

    @pl.when(here > 0)
    def _():
        prepare(1)

    @pl.when(here == 0)
    def _():
        for copy in x_in:
            copy.wait()

    x_done = forward_items(
        here, sections, right, lambda: prepare(1), wa, wb, xs, xout, ps, invs, xsend, xrecv
    )

    @pl.when(here == sections - 1)
    def _():
        for copy in g_in:
            copy.wait()

    x_done()
    late_item, late_done = backward_items(
        here, sections, left, 1, wa, wb, xs, ps, invs, gs, xout, gpis, hs, gsend, grecv
    )
    lax.fori_loop(0, batches, late_item, 0)
    weight_terms(batches, xs, gs, gpis, hs, turned, later)
    late_begin, late_step, late_end, late_drain = ring(
        me, groups, later, late_slots, late_send, late_recv
    )
    begin, step, end, drain = ring(me, groups, stage, slots, rsend, rrecv)
    late_begin()
    item, done = backward_items(
        here, sections, left, 0, wa, wb, xs, ps, invs, gs, xout, gpis, hs, gsend, grecv
    )
    turns = batches + sections - 1

    def turn(t, _):
        i = t - (sections - 1 - here)

        @pl.when((i >= 0) & (i < batches))
        def _():
            item(jnp.clip(i, 0, batches - 1), 0)

        @pl.when(t + 1 <= groups - 2)
        def _():
            late_step(jnp.minimum(t + 1, groups - 2))

        return 0

    lax.fori_loop(0, turns, turn, 0)
    for k in range(turns + 1, groups - 1):
        late_step(jnp.int32(k))
    weight_terms(0, xs, gs, gpis, hs, turned, stage)
    begin()
    late_end(totals)
    late_out = pltpu.make_async_copy(totals, out.at[1], out_sem.at[0])
    late_out.start()

    def walk(k, _):
        step(k)
        return 0

    lax.fori_loop(1, groups - 1, walk, 0)
    late_out.wait()
    end(totals)
    last_out = pltpu.make_async_copy(totals, out.at[0], out_sem.at[1])
    last_out.start()
    late_done()
    done()
    late_drain()
    drain()
    last_out.wait()


def expand_blocks(mask):
    return jnp.repeat(jnp.repeat(mask, BLK, axis=-2), BLK, axis=-1)


def on_device(micro_inputs, out_cotangent, weight_a, weight_b, mask_a, mask_b):
    sections = lax.axis_size("section")
    groups = lax.axis_size("dp")
    owner = lax.axis_index("dp")
    batches, tokens, width = micro_inputs.shape
    inner = weight_a.shape[3]
    span = width // groups
    wide = width // CHUNKS
    rows_a = jnp.repeat(mask_a[:, 0].astype(F32), BLK, axis=-1)
    cols_b = jnp.repeat(mask_b[:, 0].astype(F32), BLK, axis=-1)
    any_spec = pl.BlockSpec(memory_space=pl.ANY)
    vmem_spec = pl.BlockSpec(memory_space=pltpu.VMEM)
    dma = pltpu.SemaphoreType.DMA
    block = (CHUNKS, tokens, wide)
    ring_slots = (2, groups - 1, 2, inner // 2, span)
    flops = 2 * batches * tokens * width * inner
    totals = pl.pallas_call(
        functools.partial(whole_kernel, sections, groups),
        out_shape=jax.ShapeDtypeStruct((2, 2, inner, span), F32),
        in_specs=[any_spec] * 4 + [vmem_spec] * 2,
        out_specs=any_spec,
        scratch_shapes=[
            pltpu.VMEM((2, width, inner), BF16),
            pltpu.VMEM((2, inner, width), BF16),
            pltpu.VMEM((2 * batches,) + block, BF16),
            pltpu.VMEM((2 * batches,) + block, BF16),
            pltpu.VMEM((2 * batches, tokens, inner), F32),
            pltpu.VMEM((2 * batches, tokens, 128), F32),
            pltpu.VMEM((2 * batches,) + block, BF16),
            pltpu.VMEM((batches, tokens, inner), BF16),
            pltpu.VMEM((batches, tokens, inner), BF16),
            pltpu.VMEM((inner, batches * tokens), BF16),
            pltpu.VMEM((2, groups, inner, span), BF16),
            pltpu.VMEM((2, groups, inner, span), BF16),
            pltpu.VMEM(ring_slots, BF16),
            pltpu.VMEM(ring_slots, BF16),
            pltpu.VMEM((2, inner, span), F32),
            dma((4 + 2 * CHUNKS,)),
            dma((2 * batches, CHUNKS)),
            dma((2 * batches, CHUNKS)),
            dma((2 * batches, CHUNKS)),
            dma((2 * batches, CHUNKS)),
            dma(ring_slots[:3]),
            dma(ring_slots[:3]),
            dma(ring_slots[:3]),
            dma(ring_slots[:3]),
            dma((2,)),
        ],
        compiler_params=pltpu.CompilerParams(
            collective_id=0, has_side_effects=True, vmem_limit_bytes=LIMIT
        ),
        cost_estimate=pl.CostEstimate(
            flops=12 * flops, bytes_accessed=40 * 1024 * 1024, transcendentals=0
        ),
    )(micro_inputs, out_cotangent, weight_a, weight_b, rows_a, cols_b)

    def settle(lap):
        held = span // BLK
        own_a = expand_blocks(lax.dynamic_slice_in_dim(mask_a[lap, 0], owner * held, held, 0))
        own_b = expand_blocks(lax.dynamic_slice_in_dim(mask_b[lap, 0], owner * held, held, 1))
        return jnp.transpose(totals[lap, 0]) * own_a.astype(F32), totals[lap, 1] * own_b.astype(F32)

    later_zero = settle(0)
    later_one = settle(1)
    grad_a = jnp.stack([later_zero[0], later_one[0]])[:, None]
    grad_b = jnp.stack([later_zero[1], later_one[1]])[:, None]
    return (grad_a, grad_b)


def solution(mesh):
    placed = (
        P(None, "dp", None),
        P(None, "dp", None),
        P(None, "section", None, None),
        P(None, "section", None, None),
        P(None, "section", None, None),
        P(None, "section", None, None),
    )
    return jax.shard_map(
        on_device,
        mesh=mesh,
        in_specs=placed,
        out_specs=(P(None, "section", "dp", None), P(None, "section", None, "dp")),
        check_vma=False,
    )
```

```python
import functools

import jax
import jax.numpy as jnp
from jax import lax
from jax.experimental import pallas as pl
from jax.experimental.pallas import tpu as pltpu
from jax.sharding import PartitionSpec as P

BLK = 64
EPS = 1e-05
CHUNKS = 4
LIMIT = 64 * 1024 * 1024 - 64 * 1024
MESH = pl.DeviceIdType.MESH
NT = (((1,), (1,)), ((), ()))
F32 = jnp.float32
BF16 = jnp.bfloat16


def mask_up(wa, lap, rows_a):
    def body(b, _):
        rows = pl.ds(pl.multiple_of(b * BLK, BLK), BLK)
        keep = rows_a[lap, pl.ds(b, 1), :].astype(BF16)
        wa[lap, rows, :] = wa[lap, rows, :] * keep
        return 0

    lax.fori_loop(0, wa.shape[1] // BLK, body, 0)


def mask_down(wb, lap, cols_b):
    def body(b, _):
        rows = pl.ds(pl.multiple_of(b * BLK, BLK), BLK)
        keep = cols_b[lap, pl.ds(b, 1), :].astype(BF16)
        wb[lap, rows, :] = wb[lap, rows, :] * keep
        return 0

    lax.fori_loop(0, wb.shape[1] // BLK, body, 0)


def chunk_copies(src, dst, sems, base):
    wide = src.shape[-1] // CHUNKS
    return [
        pltpu.make_async_copy(src.at[:, :, pl.ds(c * wide, wide)], dst.at[:, c], sems.at[base + c])
        for c in range(CHUNKS)
    ]


def forward_items(here, sections, right, prepare, wa, wb, xs, xout, ps, invs, send, recv):
    batches = xs.shape[0] // 2
    wide = xs.shape[-1]
    width = wide * CHUNKS

    def hop(i, c):
        last = here == sections - 1
        slot = jnp.minimum(i + jnp.where(last, batches, 0), 2 * batches - 1)
        return pltpu.make_async_remote_copy(
            src_ref=xout.at[i, c],
            dst_ref=xs.at[slot, c],
            send_sem=send.at[i, c],
            recv_sem=recv.at[slot, c],
            device_id={"section": right},
            device_id_type=MESH,
        )

    def landed(i, c):
        return pltpu.make_async_remote_copy(
            src_ref=xout.at[i, c],
            dst_ref=xs.at[i, c],
            send_sem=send.at[i, c],
            recv_sem=recv.at[i, c],
            device_id={"section": right},
            device_id_type=MESH,
        )

    def item(i, _):
        lap = i // batches
        from_left = (here > 0) | (lap > 0)
        go_on = (here < sections - 1) | (lap == 0)

        @pl.when((here == 0) & (i == batches))
        def _():
            prepare()

        total = None
        square = None
        for c in range(CHUNKS):

            @pl.when(from_left)
            def _():
                landed(i, c).wait_recv()

            x = xs[i, c]
            xf = x.astype(F32)
            sq = jnp.sum(xf * xf, axis=-1, keepdims=True)
            q = jnp.dot(x, wa[lap, pl.ds(c * wide, wide), :], preferred_element_type=F32)
            total = q if total is None else total + q
            square = sq if square is None else square + sq
        inv = lax.rsqrt(square / width + EPS)
        p = total * inv
        ps[i] = p
        invs[i] = jnp.broadcast_to(inv, invs.shape[1:])

        @pl.when(go_on)
        def _():
            h = (p * jax.nn.sigmoid(p)).astype(BF16)
            for c in range(CHUNKS):
                y = jnp.dot(h, wb[lap, :, pl.ds(c * wide, wide)], preferred_element_type=F32)
                xout[i, c] = (xs[i, c].astype(F32) + y).astype(BF16)
                hop(i, c).start()

        return 0

    lax.fori_loop(0, 2 * batches, item, 0)

    def finish():
        def body(i, _):
            lap = i // batches

            @pl.when((here < sections - 1) | (lap == 0))
            def _():
                for c in range(CHUNKS):
                    hop(i, c).wait_send()

            return 0

        lax.fori_loop(0, 2 * batches, body, 0)

    return finish


def backward_items(here, sections, left, lap, wa, wb, xs, ps, invs, gs, gout, gpis, hs, send, recv):
    batches = gpis.shape[0]
    wide = gs.shape[-1]
    width = wide * CHUNKS
    base = lap * batches

    def hop(i, c):
        slot = base + i
        if lap:
            slot = slot - jnp.where(here == 0, batches, 0)
        return pltpu.make_async_remote_copy(
            src_ref=gout.at[base + i, c],
            dst_ref=gs.at[slot, c],
            send_sem=send.at[base + i, c],
            recv_sem=recv.at[slot, c],
            device_id={"section": left},
            device_id_type=MESH,
        )

    def landed(i, c):
        return pltpu.make_async_remote_copy(
            src_ref=gout.at[base + i, c],
            dst_ref=gs.at[base + i, c],
            send_sem=send.at[base + i, c],
            recv_sem=recv.at[base + i, c],
            device_id={"section": left},
            device_id_type=MESH,
        )

    def item(i, _):
        total = None
        for c in range(CHUNKS):
            if lap:

                @pl.when(here < sections - 1)
                def _():
                    landed(i, c).wait_recv()

            else:
                landed(i, c).wait_recv()
            q = lax.dot_general(
                gs[base + i, c], wb[lap, :, pl.ds(c * wide, wide)], NT, preferred_element_type=F32
            )
            total = q if total is None else total + q
        p = ps[base + i]
        inv = invs[base + i][:, :1]
        sg = jax.nn.sigmoid(p)
        gp = total * sg * (1.0 + p * (1.0 - sg))
        rounded = gp.astype(BF16)
        gpis[i] = (gp * inv).astype(BF16)
        hs[i] = (p * sg).astype(BF16)
        mean = jnp.sum(rounded.astype(F32) * p, axis=-1, keepdims=True) / width
        scale = inv * inv * mean

        def outgoing():
            for c in range(CHUNKS):
                gn = lax.dot_general(
                    rounded, wa[lap, pl.ds(c * wide, wide), :], NT, preferred_element_type=F32
                )
                out = gs[base + i, c].astype(F32) + inv * gn - xs[base + i, c].astype(F32) * scale
                gout[base + i, c] = out.astype(BF16)
                hop(i, c).start()

        if lap:
            outgoing()
        else:
            pl.when(here > 0)(outgoing)
        return 0

    def finish():
        def body(i, _):
            for c in range(CHUNKS):
                if lap:
                    hop(i, c).wait_send()
                else:

                    @pl.when(here > 0)
                    def _():
                        hop(i, c).wait_send()

            return 0

        lax.fori_loop(0, batches, body, 0)

    return item, finish


def weight_terms(base, xs, gs, gpis, hs, turned, stage, begin):
    batches = gpis.shape[0]
    wide = gs.shape[-1]
    tokens = gs.shape[2]
    rows = batches * tokens
    groups, inner, span = stage.shape[1:]
    per = wide // span
    for part, (left, right) in enumerate(((gpis, xs), (hs, gs))):
        turned[...] = jnp.transpose(left[...].astype(F32).reshape(rows, inner)).astype(BF16)

        def owner(c, _):
            for k in range(per):
                block = right[pl.ds(base, batches), c, :, pl.ds(k * span, span)].reshape(rows, span)
                stage[part, c * per + k] = jnp.dot(
                    turned[...], block, preferred_element_type=F32
                ).astype(BF16)
            return 0

        lax.fori_loop(0, CHUNKS, owner, 0)
        begin(part)


def ring(me, groups, stage, slots, sends, recvs):
    half = stage.shape[2] // 2
    place = jnp.where(me % 2 == 0, me // 2, groups - 1 - me // 2)

    def device_at(spot):
        return jnp.where(spot < groups // 2, 2 * spot, 2 * (groups - 1 - spot) + 1)

    def peer(way):
        return device_at(lax.rem(place + (1 if way == 0 else groups - 1), groups))

    def own(way, part, k):
        spot = place + 2 * groups - 1 - k if way == 0 else place + 1 + k
        return stage.at[part, device_at(lax.rem(spot, groups)), pl.ds(way * half, half)]

    def hop(way, part, k):
        return pltpu.make_async_remote_copy(
            src_ref=slots.at[way, jnp.maximum(k - 1, 0), part],
            dst_ref=slots.at[way, k, part],
            send_sem=sends.at[way, k, part],
            recv_sem=recvs.at[way, k, part],
            device_id={"dp": peer(way)},
            device_id_type=MESH,
        )

    def first(way, part):
        return pltpu.make_async_remote_copy(
            src_ref=own(way, part, 0),
            dst_ref=slots.at[way, 0, part],
            send_sem=sends.at[way, 0, part],
            recv_sem=recvs.at[way, 0, part],
            device_id={"dp": peer(way)},
            device_id_type=MESH,
        )

    pairs = [(way, part) for part in range(2) for way in range(2)]

    def begin(part):
        for way in range(2):
            first(way, part).start()

    def step(k):
        for way, part in pairs:
            hop(way, part, k - 1).wait_recv()
            term = own(way, part, k)[...].astype(F32)
            slot = slots.at[way, k - 1, part]
            slot[...] = (slot[...].astype(F32) + term).astype(BF16)
            hop(way, part, k).start()

    def end(total):
        for way, part in pairs:
            hop(way, part, groups - 2).wait_recv()
            term = own(way, part, groups - 1)[...].astype(F32)
            total[part, pl.ds(way * half, half)] = (
                slots[way, groups - 2, part].astype(F32) + term
            )

    def drain():
        for way, part in pairs:
            first(way, part).wait_send()

        def body(k, _):
            for way, part in pairs:
                hop(way, part, k).wait_send()
            return 0

        lax.fori_loop(1, groups - 1, body, 0)

    return begin, step, end, drain


def whole_kernel(
    sections, groups, micro, cot, weight_a, weight_b, rows_a, cols_b,
    out,
    wa, wb, xs, xout, ps, invs, gs, gpis, hs, turned, stage, later, slots, late_slots, totals,
    load, xsend, xrecv, gsend, grecv, rsend, rrecv, late_send, late_recv, out_sem,
):
    here = lax.axis_index("section")
    me = lax.axis_index("dp")
    batches = gpis.shape[0]
    loads = []
    for lap in range(2):
        loads.append(pltpu.make_async_copy(weight_a.at[lap, 0], wa.at[lap], load.at[2 * lap]))
        loads.append(pltpu.make_async_copy(weight_b.at[lap, 0], wb.at[lap], load.at[2 * lap + 1]))
    x_in = chunk_copies(micro, xs.at[pl.ds(0, batches)], load, 4)
    g_in = chunk_copies(cot, gs.at[pl.ds(batches, batches)], load, 4 + CHUNKS)
    loads[0].start()

    @pl.when(here == 0)
    def _():
        for copy in x_in:
            copy.start()

    for copy in loads[1:]:
        copy.start()

    @pl.when(here == sections - 1)
    def _():
        for copy in g_in:
            copy.start()

    barrier = pltpu.get_barrier_semaphore()
    place = jnp.where(me % 2 == 0, me // 2, groups - 1 - me // 2)
    right = lax.rem(here + 1, sections)
    left = lax.rem(here + sections - 1, sections)
    for away in (1, groups - 1):
        spot = lax.rem(place + away, groups)
        other = jnp.where(spot < groups // 2, 2 * spot, 2 * (groups - 1 - spot) + 1)
        pl.semaphore_signal(barrier, inc=1, device_id={"dp": other}, device_id_type=MESH)
    for other in (left, right):
        pl.semaphore_signal(barrier, inc=1, device_id={"section": other}, device_id_type=MESH)
    pl.semaphore_wait(barrier, 4)

    def prepare(lap):
        loads[2 * lap].wait()
        mask_up(wa, lap, rows_a)
        loads[2 * lap + 1].wait()
        mask_down(wb, lap, cols_b)

    prepare(0)

    @pl.when(here > 0)
    def _():
        prepare(1)

    @pl.when(here == 0)
    def _():
        for copy in x_in:
            copy.wait()

    x_done = forward_items(
        here, sections, right, lambda: prepare(1), wa, wb, xs, xout, ps, invs, xsend, xrecv
    )

    @pl.when(here == sections - 1)
    def _():
        for copy in g_in:
            copy.wait()

    x_done()
    late_item, late_done = backward_items(
        here, sections, left, 1, wa, wb, xs, ps, invs, gs, xout, gpis, hs, gsend, grecv
    )
    lax.fori_loop(0, batches, late_item, 0)
    late_begin, late_step, late_end, late_drain = ring(
        me, groups, later, late_slots, late_send, late_recv
    )
    begin, step, end, drain = ring(me, groups, stage, slots, rsend, rrecv)
    weight_terms(batches, xs, gs, gpis, hs, turned, later, late_begin)
    item, done = backward_items(
        here, sections, left, 0, wa, wb, xs, ps, invs, gs, xout, gpis, hs, gsend, grecv
    )
    turns = max(batches + 1, groups - 2)

    def turn(t, _):
        i = t - 1

        @pl.when((i >= 0) & (i < batches))
        def _():
            item(jnp.clip(i, 0, batches - 1), 0)

        @pl.when(t + 1 <= groups - 2)
        def _():
            late_step(jnp.minimum(t + 1, groups - 2))

        return 0

    lax.fori_loop(0, turns, turn, 0)
    weight_terms(0, xs, gs, gpis, hs, turned, stage, begin)
    late_end(totals)
    late_out = pltpu.make_async_copy(totals, out.at[1], out_sem.at[0])
    late_out.start()

    def walk(k, _):
        step(k)
        return 0

    lax.fori_loop(1, groups - 1, walk, 0)
    late_out.wait()
    end(totals)
    last_out = pltpu.make_async_copy(totals, out.at[0], out_sem.at[1])
    last_out.start()
    late_done()
    done()
    late_drain()
    drain()
    last_out.wait()


def expand_blocks(mask):
    return jnp.repeat(jnp.repeat(mask, BLK, axis=-2), BLK, axis=-1)


def on_device(micro_inputs, out_cotangent, weight_a, weight_b, mask_a, mask_b):
    sections = lax.axis_size("section")
    groups = lax.axis_size("dp")
    owner = lax.axis_index("dp")
    batches, tokens, width = micro_inputs.shape
    inner = weight_a.shape[3]
    span = width // groups
    wide = width // CHUNKS
    rows_a = jnp.repeat(mask_a[:, 0].astype(F32), BLK, axis=-1)
    cols_b = jnp.repeat(mask_b[:, 0].astype(F32), BLK, axis=-1)
    any_spec = pl.BlockSpec(memory_space=pl.ANY)
    vmem_spec = pl.BlockSpec(memory_space=pltpu.VMEM)
    dma = pltpu.SemaphoreType.DMA
    block = (CHUNKS, tokens, wide)
    ring_slots = (2, groups - 1, 2, inner // 2, span)
    flops = 2 * batches * tokens * width * inner
    totals = pl.pallas_call(
        functools.partial(whole_kernel, sections, groups),
        out_shape=jax.ShapeDtypeStruct((2, 2, inner, span), F32),
        in_specs=[any_spec] * 4 + [vmem_spec] * 2,
        out_specs=any_spec,
        scratch_shapes=[
            pltpu.VMEM((2, width, inner), BF16),
            pltpu.VMEM((2, inner, width), BF16),
            pltpu.VMEM((2 * batches,) + block, BF16),
            pltpu.VMEM((2 * batches,) + block, BF16),
            pltpu.VMEM((2 * batches, tokens, inner), F32),
            pltpu.VMEM((2 * batches, tokens, 128), F32),
            pltpu.VMEM((2 * batches,) + block, BF16),
            pltpu.VMEM((batches, tokens, inner), BF16),
            pltpu.VMEM((batches, tokens, inner), BF16),
            pltpu.VMEM((inner, batches * tokens), BF16),
            pltpu.VMEM((2, groups, inner, span), BF16),
            pltpu.VMEM((2, groups, inner, span), BF16),
            pltpu.VMEM(ring_slots, BF16),
            pltpu.VMEM(ring_slots, BF16),
            pltpu.VMEM((2, inner, span), F32),
            dma((4 + 2 * CHUNKS,)),
            dma((2 * batches, CHUNKS)),
            dma((2 * batches, CHUNKS)),
            dma((2 * batches, CHUNKS)),
            dma((2 * batches, CHUNKS)),
            dma(ring_slots[:3]),
            dma(ring_slots[:3]),
            dma(ring_slots[:3]),
            dma(ring_slots[:3]),
            dma((2,)),
        ],
        compiler_params=pltpu.CompilerParams(
            collective_id=0, has_side_effects=True, vmem_limit_bytes=LIMIT
        ),
        cost_estimate=pl.CostEstimate(
            flops=12 * flops, bytes_accessed=40 * 1024 * 1024, transcendentals=0
        ),
    )(micro_inputs, out_cotangent, weight_a, weight_b, rows_a, cols_b)

    def settle(lap):
        held = span // BLK
        own_a = expand_blocks(lax.dynamic_slice_in_dim(mask_a[lap, 0], owner * held, held, 0))
        own_b = expand_blocks(lax.dynamic_slice_in_dim(mask_b[lap, 0], owner * held, held, 1))
        return jnp.transpose(totals[lap, 0]) * own_a.astype(F32), totals[lap, 1] * own_b.astype(F32)

    later_zero = settle(0)
    later_one = settle(1)
    grad_a = jnp.stack([later_zero[0], later_one[0]])[:, None]
    grad_b = jnp.stack([later_zero[1], later_one[1]])[:, None]
    return (grad_a, grad_b)


def solution(mesh):
    placed = (
        P(None, "dp", None),
        P(None, "dp", None),
        P(None, "section", None, None),
        P(None, "section", None, None),
        P(None, "section", None, None),
        P(None, "section", None, None),
    )
    return jax.shard_map(
        on_device,
        mesh=mesh,
        in_specs=placed,
        out_specs=(P(None, "section", "dp", None), P(None, "section", None, "dp")),
        check_vma=False,
    )
```
